32 devices in a mesh: groups: 1, rail: 16 (over z, y, x), node: 2 (over core).
Axes of the slice: x: 2, y: 2, z: 4, core: 2. Of those that a mesh axis runs over, the one named last changes fastest.
Arguments:
- tokens: bfloat16 [512, 7168], P(('groups', 'rail', 'node')), may hold values from -6 to 6
- routes: int32 [512, 2], P(('groups', 'rail', 'node')), may hold values from 0 to 3, all different within a row; in each aligned block of 16 rows (0 to 15, 16 to 31, ...) at most 12 rows name the same one
- route_weight: int32 [512, 2], P(('groups', 'rail', 'node')), may hold values from 1 to 255
- gate_weight: bfloat16 [16, 2, 7168, 256], P('rail', 'node'), may hold values from -0.0625 to 0.0625
- up_weight: bfloat16 [16, 2, 7168, 256], P('rail', 'node'), may hold values from -0.0625 to 0.0625
- down_weight: bfloat16 [16, 2, 256, 7168], P('rail', 'node'), may hold values from -0.125 to 0.125
Outputs:
- moe_out: bfloat16 [512, 7168], P(('groups', 'rail', 'node'))
The draws below stay inside these ranges and needn't reach their ends.
Inputs may be any that keep to these rules, and one draw needn't show every extreme that they name: `routes`: each row names 2 different experts; among the 16 rows of one device no expert is named by more than 12 rows, and in some blocks of every draw an expert is named by exactly 12.
All inputs are finite; a program needn't handle non-finite values.
Results may differ from the reference program's by a relative error of at most 0.0085.
Values may be sent and summed in bfloat16 or wider, within the bound.
A program may use at most 128 MiB of HBM per device.

```python
import math
import jax
import jax.numpy as jnp
import numpy as np
from jax import lax

D = 7168
HID = 2048
SLICES = 8
TOP = 2
TOK_DEV = 16
EXPERTS = 4
CAP = 12
TOKENS = 512
N_RAIL = 16
N_NODE = 2


def place_ends(entries, rng, smallest, high):
    longest = entries.shape.index(max(entries.shape))
    spots = []
    for shift in (0, 1):
        where = [jax.random.randint(jax.random.fold_in(rng, axis), (), 0, length) for axis, length in enumerate(entries.shape)]
        where[longest] = (where[longest] + shift) % entries.shape[longest]
        spots.append(tuple(where))
    return entries.at[spots[0]].set(smallest).at[spots[1]].set(high)


def block_levels(rng, extent, split, low, largest):
    level, own = 1.0, jax.random.fold_in(rng, 6)
    for axis_at, blocks in split:
        steps = jnp.exp(jax.random.uniform(jax.random.fold_in(own, axis_at), (blocks,), jnp.float32, low / len(split), largest / len(split)))
        level = level * jnp.repeat(steps, extent[axis_at] // blocks).reshape([-1 if axis == axis_at else 1 for axis in range(len(extent))])
    return level


def routed_block(key, own, number, rows, number_of, top, bound, lean):
    ranking = jax.random.permutation(key, number_of)
    packed, common = load_shares(number_of, rows * top, bound, lean, True), load_shares(number_of, rows * top, bound, lean, False)
    places = jnp.arange(number_of)

    def named(lengths, rotation):
        used = int((lengths > 0).sum())
        fixed = max(1, used // 4)
        passed = fixed + (places - fixed + rotation * (used - fixed)) % max(1, number_of - fixed)
        return jnp.zeros((number_of,), jnp.int32).at[ranking[jnp.where(places < fixed, places, passed)]].set(jnp.asarray(lengths, jnp.int32))

    lengths = jnp.where(number % 4 == 0, named(packed, number // 4), named(common, number - number // 4 - 1))
    mixed = jax.random.permutation(jax.random.fold_in(own, 3), number_of)
    giver, sink = mixed[0:number_of // 2 * 2:2], mixed[1:number_of // 2 * 2:2]
    margin = jnp.minimum(lengths[giver] - 1, bound - lengths[sink]) // 2
    margin = jnp.where((giver == ranking[0]) | (sink == ranking[0]) | (lengths[sink] == 0), 0, jnp.maximum(margin, 0))
    passed = jax.random.randint(jax.random.fold_in(own, 4), (number_of // 2,), 0, 1 << 20) % (margin + 1)
    lengths = lengths.at[giver].add(-passed).at[sink].add(passed)
    members = jnp.searchsorted(jnp.cumsum(lengths), jnp.arange(rows * top), side="right").astype(jnp.int32)
    grid = members.reshape(top, rows).T
    grid = grid[jax.random.permutation(jax.random.fold_in(own, 1), rows)]
    rotation = jax.random.randint(jax.random.fold_in(own, 2), (rows, 1), 0, top)
    return jnp.take_along_axis(grid, (jnp.arange(top)[None, :] + rotation) % top, axis=1)


def load_shares(number_of, total, bound, lean, full):
    portions = [(1 << 20) // math.isqrt(rank ** lean) + 1 for rank in range(1, number_of + 1)]
    largest = bound if full else min(bound, max(-(-total // number_of), total * portions[0] // sum(portions)))
    least = 1 if total - largest >= number_of - 1 else 0
    holding, rest = [largest] + [least] * (number_of - 1), total - largest - least * (number_of - 1)
    while rest > 0:
        movable = [i for i in range(1, number_of) if holding[i] < largest] or [i for i in range(1, number_of) if holding[i] < bound]
        whole, remaining = sum([portions[i] for i in movable]), rest
        for i in movable:
            extra = min(bound - holding[i], max(1, remaining * portions[i] // whole), rest)
            holding[i] = holding[i] + extra
            rest = rest - extra
    return np.array(holding)


def gaussian(own_key, dims, deviation, limit, shards=(), held_as=jnp.bfloat16):
    entries = jax.random.normal(own_key, dims, jnp.float32) * deviation
    if len(shards) > 0:
        entries = block_levels(own_key, dims, shards, -0.22, 0.18) * entries
    return jnp.clip(entries, min=-limit, max=limit).astype(held_as)


def setup_inputs(seed: int = 0, part: int = 0) -> dict:
    streams_of = jax.random.split(jax.random.key(seed), 7)
    part_splits = jax.random.split(jax.random.fold_in(streams_of[6], part), 7)
    tokens = gaussian(part_splits[0], (TOKENS, D), 1.0, 6.0, ((0, 32),))
    routes_keys = jax.random.split(jax.random.fold_in(part_splits[1], 1), TOKENS // TOK_DEV)
    routes_turns = jax.random.permutation(jax.random.fold_in(part_splits[1], 3), TOKENS // TOK_DEV)
    routes = jax.vmap(lambda own, number: routed_block(jax.random.fold_in(part_splits[1], 2), own, number, TOK_DEV, EXPERTS, TOP, CAP, 2))(routes_keys, routes_turns).reshape((TOKENS, TOP))
    route_weight = place_ends(jax.random.randint(part_splits[2], (TOKENS, TOP), 1, 256), jax.random.fold_in(part_splits[2], 1), 1, 255).astype(jnp.int32)
    gate_weight = gaussian(streams_of[3], (N_RAIL, N_NODE, D, HID // SLICES), D ** -0.5, 0.0625, ((0, 16), (1, 2)))
    up_weight = gaussian(streams_of[4], (N_RAIL, N_NODE, D, HID // SLICES), D ** -0.5, 0.0625, ((0, 16), (1, 2)))
    down_weight = gaussian(streams_of[5], (N_RAIL, N_NODE, HID // SLICES, D), HID ** -0.5, 0.125, ((0, 16), (1, 2)))
    return {"tokens": tokens, "routes": routes, "route_weight": route_weight, "gate_weight": gate_weight, "up_weight": up_weight, "down_weight": down_weight}


def slot_numbers(routes):
    blocks = routes.reshape(-1, TOK_DEV * TOP)
    onehot = (blocks[:, :, None] == jnp.arange(EXPERTS, dtype=jnp.int32)[None, None, :]).astype(jnp.int32)
    earlier = jnp.cumsum(onehot, axis=1) - onehot
    return jnp.sum(earlier * onehot, axis=2).astype(jnp.int32)


def arrange(weight):
    split_count = N_RAIL // SLICES
    shaped = weight.reshape(split_count, SLICES, N_NODE, weight.shape[2], weight.shape[3])
    return shaped.transpose(0, 2, 1, 3, 4).reshape(EXPERTS, SLICES, weight.shape[2], weight.shape[3])


def reference(tokens, routes, route_weight, gate_weight, up_weight, down_weight):
    block_count = TOKENS // TOK_DEV
    slot_of = slot_numbers(routes)
    local_row = jnp.broadcast_to((jnp.arange(TOK_DEV * TOP, dtype=jnp.int32) // TOP)[None, :], slot_of.shape)
    block_ids = jnp.broadcast_to(jnp.arange(block_count, dtype=jnp.int32)[:, None], slot_of.shape)
    token_of = jnp.zeros((EXPERTS, block_count, CAP), jnp.int32)
    token_of = token_of.at[routes.reshape(block_count, -1), block_ids, slot_of].set(local_row + 1)

    def expert_rows(items):
        owner, w_gate, w_up, w_down = items
        global_row = jnp.arange(block_count, dtype=jnp.int32)[:, None] * TOK_DEV + owner - 1
        picked = tokens[jnp.maximum(global_row, 0)]
        inputs = jnp.where((owner > 0)[:, :, None], picked, jnp.zeros((), tokens.dtype)).reshape(-1, D)
        wide = inputs.astype(jnp.float32)
        gate_vals = jnp.einsum("rd,sdh->srh", wide, w_gate.astype(jnp.float32))
        up_vals = jnp.einsum("rd,sdh->srh", wide, w_up.astype(jnp.float32))
        hidden = (jax.nn.silu(gate_vals) * up_vals).astype(jnp.bfloat16)
        partial_value = jnp.einsum("srh,shd->srd", hidden.astype(jnp.float32), w_down.astype(jnp.float32))
        summed = jnp.sum(partial_value, axis=0)
        return summed.reshape(block_count, CAP, D)

    results = lax.map(expert_rows, (token_of, arrange(gate_weight), arrange(up_weight), arrange(down_weight)))
    block_of = (jnp.arange(TOKENS, dtype=jnp.int32) // TOK_DEV)[:, None]
    chosen = results[routes, block_of, slot_of.reshape(TOKENS, TOP)]
    share = route_weight.astype(jnp.float32) / 256.0
    return jnp.sum(share[:, :, None] * chosen, axis=1).astype(jnp.bfloat16)
```

```python
import functools

import jax
import jax.numpy as jnp
from jax import lax
from jax.experimental import pallas as pl
from jax.experimental.pallas import tpu as pltpu
from jax.sharding import PartitionSpec as P

SLICES = 8
SQUARE = 4
LANES = 128


def body(
    rail_size,
    node_size,
    tokens_ref,
    routes_ref,
    weight_ref,
    gate_hbm,
    up_hbm,
    down_hbm,
    out_ref,
    rows_ref,
    gate_ref,
    up_ref,
    down_ref,
    sib_buf,
    side_buf,
    line_buf,
    above_buf,
    below_buf,
    load_sem,
    chain_send,
    chain_recv,
    first_send,
    first_recv,
    second_send,
    second_recv,
    relay_send,
    relay_recv,
    sib_send,
    sib_recv,
    give_send,
    give_recv,
    side_send,
    side_recv,
    line_send,
    line_recv,
    sum_send,
    above_recv,
    below_recv,
):
    count, width = tokens_ref.shape
    middle = width // LANES // 2 * LANES
    depth = rail_size // SQUARE
    rail = lax.axis_index("rail")
    node = lax.axis_index("node")
    x, y, z = lax.rem(rail, 2), lax.rem(rail // 2, 2), rail // SQUARE
    expert = rail // SLICES * node_size + node
    to_sib = {"node": 1 - node}
    to_x = {"rail": rail + 1 - 2 * x}
    to_y = {"rail": rail + 2 - 4 * y}
    to_above = {"rail": rail + SQUARE}
    to_below = {"rail": rail - SQUARE}
    has_above = z < depth - 1
    has_below = z > 0
    steps = 2 * depth - 1

    def index_of(zz, flip_x, flip_y):
        xx = 1 - x if flip_x else x
        yy = 1 - y if flip_y else y
        return zz * SQUARE + yy * 2 + xx

    def band(i):
        return pl.ds(pl.multiple_of(i * count, count), count)

    full = slice(0, width + LANES)
    plain = slice(0, width)
    halves_wide = (slice(0, middle), slice(middle, width + LANES))
    halves = (slice(0, middle), slice(middle, width))

    def rows_at(r, n, columns):
        return rows_ref.at[band(r * node_size + n), columns]

    def copy(src, dst, send, recv, target):
        return pltpu.make_async_remote_copy(
            src_ref=src,
            dst_ref=dst,
            send_sem=send,
            recv_sem=recv,
            device_id=target,
            device_id_type=pl.DeviceIdType.MESH,
        )

    loads = [
        pltpu.make_async_copy(hbm.at[0, 0], ref, load_sem.at[i])
        for i, (hbm, ref) in enumerate(
            ((gate_hbm, gate_ref), (up_hbm, up_ref), (down_hbm, down_ref))
        )
    ]

    barrier = pltpu.get_barrier_semaphore()
    for target in (to_sib, to_x, to_y):
        pl.semaphore_signal(barrier, inc=1, device_id=target, device_id_type=pl.DeviceIdType.MESH)

    @pl.when(has_above)
    def _():
        pl.semaphore_signal(
            barrier, inc=1, device_id=to_above, device_id_type=pl.DeviceIdType.MESH
        )

    @pl.when(has_below)
    def _():
        pl.semaphore_signal(
            barrier, inc=1, device_id=to_below, device_id_type=pl.DeviceIdType.MESH
        )

    own = band(rail * node_size + node)
    rows_ref[own, plain] = tokens_ref[...]
    lane = lax.broadcasted_iota(jnp.int32, (count, LANES), 1)
    named = jnp.zeros((count, LANES), jnp.float32)
    for k in range(routes_ref.shape[1]):
        named += jnp.where(
            lane == routes_ref[:, k : k + 1], weight_ref[:, k : k + 1].astype(jnp.float32), 0.0
        )
    rows_ref[own, slice(width, width + LANES)] = named.astype(jnp.bfloat16)
    pl.semaphore_wait(barrier, 3 + has_above.astype(jnp.int32) + has_below.astype(jnp.int32))

    def place(q):
        half = (q + 1) // 2
        return jnp.where(lax.rem(q, 2) == 1, z - half, z + half)

    def visit(q, work):
        zz = place(q)

        @pl.when((q >= 0) & (q < steps) & (zz >= 0) & (zz < depth))
        def _():
            work(zz)

    def chain_up(zz):
        piece = rows_at(index_of(zz, 0, 0), node, full)
        return copy(piece, piece, chain_send.at[0, zz], chain_recv.at[zz], to_above)

    def chain_down(zz):
        piece = rows_at(index_of(zz, 0, 0), node, full)
        return copy(piece, piece, chain_send.at[1, zz], chain_recv.at[zz], to_below)

    def first(zz, h):
        piece = rows_at(index_of(zz, 0, 0), node, halves_wide[h])
        return copy(
            piece, piece, first_send.at[zz, h], first_recv.at[zz, h], (to_x, to_y)[h]
        )

    def first_in(zz, h):
        piece = rows_at(index_of(zz, h == 0, h == 1), node, halves_wide[h])
        return copy(
            piece, piece, first_send.at[zz, h], first_recv.at[zz, h], (to_x, to_y)[h]
        )

    def second(zz, h):
        piece = rows_at(index_of(zz, 0, 0), node, halves_wide[h])
        return copy(
            piece, piece, second_send.at[zz, h], second_recv.at[zz, h], (to_y, to_x)[h]
        )

    def second_in(zz, h):
        piece = rows_at(index_of(zz, h == 1, h == 0), node, halves_wide[h])
        return copy(
            piece, piece, second_send.at[zz, h], second_recv.at[zz, h], (to_y, to_x)[h]
        )

    def relay(zz, h):
        piece = rows_at(index_of(zz, h == 0, h == 1), node, halves_wide[h])
        return copy(
            piece, piece, relay_send.at[zz, h], relay_recv.at[zz, h], (to_y, to_x)[h]
        )

    def relay_in(zz, h):
        piece = rows_at(index_of(zz, 1, 1), node, halves_wide[h])
        return copy(
            piece, piece, relay_send.at[zz, h], relay_recv.at[zz, h], (to_y, to_x)[h]
        )

    def sibling(r):
        piece = rows_at(r, node, full)
        return copy(piece, piece, sib_send.at[r], sib_recv.at[r], to_sib)

    def sibling_in(r):
        piece = rows_at(r, 1 - node, full)
        return copy(piece, piece, sib_send.at[r], sib_recv.at[r], to_sib)

    def gather_a(zz):
        @pl.when(zz != z)
        def _():
            chain_up(zz).wait_recv()

        @pl.when((zz <= z) & has_above)
        def _():
            chain_up(zz).start()

        @pl.when((zz >= z) & has_below)
        def _():
            chain_down(zz).start()

        for h in range(2):
            first(zz, h).start()
        for h in range(2):
            second(zz, h).start()
        sibling(index_of(zz, 0, 0)).start()

    def gather_b(zz):
        for h in range(2):
            first_in(zz, h).wait_recv()
            relay(zz, h).start()

    def gather_c(zz):
        for h in range(2):
            second_in(zz, h).wait_recv()
        sibling(index_of(zz, 0, 1)).start()
        sibling(index_of(zz, 1, 0)).start()
        for h in range(2):
            relay_in(zz, h).wait_recv()
        sibling(index_of(zz, 1, 1)).start()

    def gather_step(t, carry):
        visit(t, gather_a)

        @pl.when(t == 0)
        def _():
            for load in loads:
                load.start()

        visit(t - 2, gather_b)
        visit(t - 4, gather_c)
        return carry

    lax.fori_loop(0, steps + 4, gather_step, 0)

    def gather_end(zz, carry):
        @pl.when((zz <= z) & has_above)
        def _():
            chain_up(zz).wait_send()

        @pl.when((zz >= z) & has_below)
        def _():
            chain_down(zz).wait_send()

        for h in range(2):
            first(zz, h).wait_send()
            second(zz, h).wait_send()
            relay(zz, h).wait_send()
        for fx, fy in ((0, 0), (0, 1), (1, 0), (1, 1)):
            r = index_of(zz, fx, fy)
            sibling(r).wait_send()
            sibling_in(r).wait_recv()
        return carry

    lax.fori_loop(0, depth, gather_end, 0)
    for load in loads:
        load.wait()

    total = rail_size * node_size * count
    chunk = min(128, total)
    column_step = next(s for s in (1792, 1024, 512, 256, 128) if width % s == 0)

    def compute(i, carry):
        here = pl.ds(pl.multiple_of(i * chunk, chunk), chunk)
        lane = lax.broadcasted_iota(jnp.int32, (chunk, LANES), 1)
        marks = rows_ref[here, slice(width, width + LANES)].astype(jnp.float32)
        share = jnp.sum(jnp.where(lane == expert, marks, 0.0), axis=1, keepdims=True) / 256.0
        block = rows_ref[here, plain]
        gate = jnp.dot(block, gate_ref[...], preferred_element_type=jnp.float32)
        up = jnp.dot(block, up_ref[...], preferred_element_type=jnp.float32)
        hidden = gate / (1.0 + jnp.exp(-gate)) * up * share
        hidden = hidden.astype(jnp.bfloat16)
        for low in range(0, width, column_step):
            columns = slice(low, low + column_step)
            rows_ref[here, columns] = jnp.dot(
                hidden, down_ref[:, columns], preferred_element_type=jnp.float32
            ).astype(jnp.bfloat16)
        return carry

    lax.fori_loop(0, total // chunk, compute, 0)

    def give(r):
        return copy(
            rows_at(r, 1 - node, plain),
            sib_buf.at[band(r), :],
            give_send.at[r],
            give_recv.at[r],
            to_sib,
        )

    def side(r, h):
        return copy(
            rows_at(r, node, halves[h]),
            side_buf.at[band(r), halves[h]],
            side_send.at[r, h],
            side_recv.at[r, h],
            (to_y, to_x)[h],
        )

    def line(zz, h):
        return copy(
            rows_at(index_of(zz, h == 0, h == 1), node, halves[h]),
            line_buf.at[band(zz), halves[h]],
            line_send.at[zz, h],
            line_recv.at[zz, h],
            (to_x, to_y)[h],
        )

    def sum_up(zz):
        return copy(
            rows_at(index_of(zz, 0, 0), node, plain),
            above_buf.at[band(zz), :],
            sum_send.at[zz],
            above_recv.at[zz],
            to_above,
        )

    def sum_down(zz):
        return copy(
            rows_at(index_of(zz, 0, 0), node, plain),
            below_buf.at[band(zz), :],
            sum_send.at[zz],
            below_recv.at[zz],
            to_below,
        )

    def add(r, columns, other):
        where = band(r * node_size + node)
        rows_ref[where, columns] = (
            rows_ref[where, columns].astype(jnp.float32) + other.astype(jnp.float32)
        ).astype(jnp.bfloat16)

    corners = ((1, 1), (0, 1), (1, 0), (0, 0))

    def reduce_0(zz):
        for fx, fy in corners:
            give(index_of(zz, fx, fy)).start()

    def reduce_a(zz):
        for fx, fy in corners:
            r = index_of(zz, fx, fy)
            give(r).wait_recv()
            add(r, plain, sib_buf[band(r), :])
            if fy:
                side(r, 0).start()
            if fx:
                side(r, 1).start()

    def reduce_b(zz):
        for h in range(2):
            r = index_of(zz, h == 0, h == 1)
            side(r, h).wait_recv()
            add(r, halves[h], side_buf[band(r), halves[h]])
            line(zz, h).start()
        r = index_of(zz, 0, 0)
        for h in range(2):
            side(r, h).wait_recv()
            add(r, halves[h], side_buf[band(r), halves[h]])

    def reduce_c(zz):
        for h in range(2):
            line(zz, h).wait_recv()
        r = index_of(zz, 0, 0)
        add(r, plain, line_buf[band(zz), :])

        @pl.when((zz >= z) & has_below)
        def _():
            sum_up(zz).wait_recv()
            add(r, plain, above_buf[band(zz), :])

        @pl.when((zz <= z) & has_above)
        def _():
            sum_down(zz).wait_recv()
            add(r, plain, below_buf[band(zz), :])

        @pl.when(zz > z)
        def _():
            sum_up(zz).start()

        @pl.when(zz < z)
        def _():
            sum_down(zz).start()

    def reduce_0_step(t, carry):
        visit(steps - 1 - t, reduce_0)
        return carry

    lax.fori_loop(0, steps, reduce_0_step, 0)

    def reduce_step(t, carry):
        q = steps - 1 - t
        visit(q, reduce_a)
        visit(q + 2, reduce_b)
        visit(q + 4, reduce_c)
        return carry

    lax.fori_loop(0, steps + 4, reduce_step, 0)
    out_ref[...] = rows_ref[own, plain]

    def reduce_end(zz, carry):
        for fx, fy in corners:
            r = index_of(zz, fx, fy)
            give(r).wait_send()
            if fy:
                side(r, 0).wait_send()
            if fx:
                side(r, 1).wait_send()
        for h in range(2):
            line(zz, h).wait_send()

        @pl.when(zz > z)
        def _():
            sum_up(zz).wait_send()

        @pl.when(zz < z)
        def _():
            sum_down(zz).wait_send()

        return carry

    lax.fori_loop(0, depth, reduce_end, 0)


def shards(rail_size, node_size, tokens, routes, route_weight, gate, up, down):
    count, width = tokens.shape
    hidden = gate.shape[-1]
    depth = rail_size // SQUARE
    total = rail_size * node_size * count
    bf16 = jnp.bfloat16
    dma = pltpu.SemaphoreType.DMA
    vmem = pl.BlockSpec(memory_space=pltpu.VMEM)
    hbm = pl.BlockSpec(memory_space=pl.ANY)
    return pl.pallas_call(
        functools.partial(body, rail_size, node_size),
        out_shape=jax.ShapeDtypeStruct((count, width), bf16),
        in_specs=[vmem] * 3 + [hbm] * 3,
        out_specs=vmem,
        scratch_shapes=[
            pltpu.VMEM((total, width + LANES), bf16),
            pltpu.VMEM((width, hidden), bf16),
            pltpu.VMEM((width, hidden), bf16),
            pltpu.VMEM((hidden, width), bf16),
            pltpu.VMEM((rail_size * count, width), bf16),
            pltpu.VMEM((rail_size * count, width), bf16),
            pltpu.VMEM((depth * count, width), bf16),
            pltpu.VMEM((depth * count, width), bf16),
            pltpu.VMEM((depth * count, width), bf16),
            dma((3,)),
            dma((2, depth)),
            dma((depth,)),
            dma((depth, 2)),
            dma((depth, 2)),
            dma((depth, 2)),
            dma((depth, 2)),
            dma((depth, 2)),
            dma((depth, 2)),
            dma((rail_size,)),
            dma((rail_size,)),
            dma((rail_size,)),
            dma((rail_size,)),
            dma((rail_size, 2)),
            dma((rail_size, 2)),
            dma((depth, 2)),
            dma((depth, 2)),
            dma((depth,)),
            dma((depth,)),
            dma((depth,)),
        ],
        compiler_params=pltpu.CompilerParams(
            collective_id=0, has_side_effects=True, vmem_limit_bytes=56 * 1024 * 1024
        ),
        cost_estimate=pl.CostEstimate(
            flops=6 * total * width * hidden,
            bytes_accessed=6 * width * hidden,
            transcendentals=total * hidden,
        ),
    )(tokens, routes, route_weight, gate, up, down)


def solution(mesh):
    in_specs = (
        P(("groups", "rail", "node"), None),
        P(("groups", "rail", "node"), None),
        P(("groups", "rail", "node"), None),
        P("rail", "node", None, None),
        P("rail", "node", None, None),
        P("rail", "node", None, None),
    )
    out_specs = P(("groups", "rail", "node"), None)
    work = functools.partial(shards, mesh.shape["rail"], mesh.shape["node"])
    return jax.shard_map(work, mesh=mesh, in_specs=in_specs, out_specs=out_specs, check_vma=False)
```

```python
import functools

import jax
import jax.numpy as jnp
from jax import lax
from jax.experimental import pallas as pl
from jax.experimental.pallas import tpu as pltpu
from jax.sharding import PartitionSpec as P

SLICES = 8
SQUARE = 4
LANES = 128


def body(
    rail_size,
    node_size,
    tokens_ref,
    routes_ref,
    weight_ref,
    gate_hbm,
    up_hbm,
    down_hbm,
    out_ref,
    rows_ref,
    gate_ref,
    up_ref,
    down_ref,
    sib_buf,
    side_buf,
    line_buf,
    above_buf,
    below_buf,
    load_sem,
    chain_send,
    chain_recv,
    first_send,
    first_recv,
    second_send,
    second_recv,
    relay_send,
    relay_recv,
    sib_send,
    sib_recv,
    give_send,
    give_recv,
    side_send,
    side_recv,
    line_send,
    line_recv,
    sum_send,
    above_recv,
    below_recv,
):
    count, width = tokens_ref.shape
    middle = width // LANES // 2 * LANES
    depth = rail_size // SQUARE
    rail = lax.axis_index("rail")
    node = lax.axis_index("node")
    x, y, z = lax.rem(rail, 2), lax.rem(rail // 2, 2), rail // SQUARE
    expert = rail // SLICES * node_size + node
    to_sib = {"node": 1 - node}
    to_x = {"rail": rail + 1 - 2 * x}
    to_y = {"rail": rail + 2 - 4 * y}
    to_above = {"rail": rail + SQUARE}
    to_below = {"rail": rail - SQUARE}
    has_above = z < depth - 1
    has_below = z > 0
    steps = 2 * depth - 1

    def index_of(zz, flip_x, flip_y):
        xx = 1 - x if flip_x else x
        yy = 1 - y if flip_y else y
        return zz * SQUARE + yy * 2 + xx

    def band(i):
        return pl.ds(pl.multiple_of(i * count, count), count)

    full = slice(0, width + LANES)
    plain = slice(0, width)
    halves_wide = (slice(0, middle), slice(middle, width + LANES))
    halves = (slice(0, middle), slice(middle, width))

    def rows_at(r, n, columns):
        return rows_ref.at[band(r * node_size + n), columns]

    def copy(src, dst, send, recv, target):
        return pltpu.make_async_remote_copy(
            src_ref=src,
            dst_ref=dst,
            send_sem=send,
            recv_sem=recv,
            device_id=target,
            device_id_type=pl.DeviceIdType.MESH,
        )

    loads = [
        pltpu.make_async_copy(hbm.at[0, 0], ref, load_sem.at[i])
        for i, (hbm, ref) in enumerate(
            ((gate_hbm, gate_ref), (up_hbm, up_ref), (down_hbm, down_ref))
        )
    ]

    barrier = pltpu.get_barrier_semaphore()
    for target in (to_sib, to_x, to_y):
        pl.semaphore_signal(barrier, inc=1, device_id=target, device_id_type=pl.DeviceIdType.MESH)

    @pl.when(has_above)
    def _():
        pl.semaphore_signal(
            barrier, inc=1, device_id=to_above, device_id_type=pl.DeviceIdType.MESH
        )

    @pl.when(has_below)
    def _():
        pl.semaphore_signal(
            barrier, inc=1, device_id=to_below, device_id_type=pl.DeviceIdType.MESH
        )

    own = band(rail * node_size + node)
    rows_ref[own, plain] = tokens_ref[...]
    kind = lax.broadcasted_iota(jnp.int32, (LANES, count), 0)
    table = jnp.zeros((LANES, count), jnp.float32)
    for k in range(routes_ref.shape[0]):
        table += jnp.where(
            kind == routes_ref[k : k + 1, :], weight_ref[k : k + 1, :].astype(jnp.float32), 0.0
        )
    unit = lax.broadcasted_iota(jnp.int32, (count, count), 0) == lax.broadcasted_iota(
        jnp.int32, (count, count), 1
    )
    named = lax.dot_general(
        unit.astype(jnp.bfloat16),
        table.astype(jnp.bfloat16),
        (((1,), (1,)), ((), ())),
        preferred_element_type=jnp.float32,
    )
    rows_ref[own, slice(width, width + LANES)] = named.astype(jnp.bfloat16)
    pl.semaphore_wait(barrier, 3 + has_above.astype(jnp.int32) + has_below.astype(jnp.int32))

    def place(q):
        half = (q + 1) // 2
        return jnp.where(lax.rem(q, 2) == 1, z - half, z + half)

    def visit(q, work):
        zz = place(q)

        @pl.when((q >= 0) & (q < steps) & (zz >= 0) & (zz < depth))
        def _():
            work(zz)

    def chain_up(zz):
        piece = rows_at(index_of(zz, 0, 0), node, full)
        return copy(piece, piece, chain_send.at[0, zz], chain_recv.at[zz], to_above)

    def chain_down(zz):
        piece = rows_at(index_of(zz, 0, 0), node, full)
        return copy(piece, piece, chain_send.at[1, zz], chain_recv.at[zz], to_below)

    def first(zz, h):
        piece = rows_at(index_of(zz, 0, 0), node, halves_wide[h])
        return copy(
            piece, piece, first_send.at[zz, h], first_recv.at[zz, h], (to_x, to_y)[h]
        )

    def first_in(zz, h):
        piece = rows_at(index_of(zz, h == 0, h == 1), node, halves_wide[h])
        return copy(
            piece, piece, first_send.at[zz, h], first_recv.at[zz, h], (to_x, to_y)[h]
        )

    def second(zz, h):
        piece = rows_at(index_of(zz, 0, 0), node, halves_wide[h])
        return copy(
            piece, piece, second_send.at[zz, h], second_recv.at[zz, h], (to_y, to_x)[h]
        )

    def second_in(zz, h):
        piece = rows_at(index_of(zz, h == 1, h == 0), node, halves_wide[h])
        return copy(
            piece, piece, second_send.at[zz, h], second_recv.at[zz, h], (to_y, to_x)[h]
        )

    def relay(zz, h):
        piece = rows_at(index_of(zz, h == 0, h == 1), node, halves_wide[h])
        return copy(
            piece, piece, relay_send.at[zz, h], relay_recv.at[zz, h], (to_y, to_x)[h]
        )

    def relay_in(zz, h):
        piece = rows_at(index_of(zz, 1, 1), node, halves_wide[h])
        return copy(
            piece, piece, relay_send.at[zz, h], relay_recv.at[zz, h], (to_y, to_x)[h]
        )

    def sibling(r):
        piece = rows_at(r, node, full)
        return copy(piece, piece, sib_send.at[r], sib_recv.at[r], to_sib)

    def sibling_in(r):
        piece = rows_at(r, 1 - node, full)
        return copy(piece, piece, sib_send.at[r], sib_recv.at[r], to_sib)

    def gather_a(zz):
        @pl.when(zz != z)
        def _():
            chain_up(zz).wait_recv()

        @pl.when((zz <= z) & has_above)
        def _():
            chain_up(zz).start()

        @pl.when((zz >= z) & has_below)
        def _():
            chain_down(zz).start()

        for h in range(2):
            first(zz, h).start()
        for h in range(2):
            second(zz, h).start()
        sibling(index_of(zz, 0, 0)).start()

    def gather_b(zz):
        for h in range(2):
            first_in(zz, h).wait_recv()
            relay(zz, h).start()

    def gather_c(zz):
        for h in range(2):
            second_in(zz, h).wait_recv()
        sibling(index_of(zz, 0, 1)).start()
        sibling(index_of(zz, 1, 0)).start()
        for h in range(2):
            relay_in(zz, h).wait_recv()
        sibling(index_of(zz, 1, 1)).start()

    def give(r):
        return copy(
            rows_at(r, 1 - node, plain),
            sib_buf.at[band(r), :],
            give_send.at[r],
            give_recv.at[r],
            to_sib,
        )

    def side(r, h):
        return copy(
            rows_at(r, node, halves[h]),
            side_buf.at[band(r), halves[h]],
            side_send.at[r, h],
            side_recv.at[r, h],
            (to_y, to_x)[h],
        )

    def line(zz, h):
        return copy(
            rows_at(index_of(zz, h == 0, h == 1), node, halves[h]),
            line_buf.at[band(zz), halves[h]],
            line_send.at[zz, h],
            line_recv.at[zz, h],
            (to_x, to_y)[h],
        )

    def sum_up(zz):
        return copy(
            rows_at(index_of(zz, 0, 0), node, plain),
            above_buf.at[band(zz), :],
            sum_send.at[zz],
            above_recv.at[zz],
            to_above,
        )

    def sum_down(zz):
        return copy(
            rows_at(index_of(zz, 0, 0), node, plain),
            below_buf.at[band(zz), :],
            sum_send.at[zz],
            below_recv.at[zz],
            to_below,
        )

    def add(r, columns, other):
        where = band(r * node_size + node)
        rows_ref[where, columns] = (
            rows_ref[where, columns].astype(jnp.float32) + other.astype(jnp.float32)
        ).astype(jnp.bfloat16)

    corners = ((1, 1), (0, 1), (1, 0), (0, 0))

    def reduce_0(zz):
        for fx, fy in corners:
            give(index_of(zz, fx, fy)).start()

    def reduce_a(zz):
        for fx, fy in corners:
            r = index_of(zz, fx, fy)
            give(r).wait_recv()
            add(r, plain, sib_buf[band(r), :])
            if fy:
                side(r, 0).start()
            if fx:
                side(r, 1).start()

    def reduce_b(zz):
        for h in range(2):
            r = index_of(zz, h == 0, h == 1)
            side(r, h).wait_recv()
            add(r, halves[h], side_buf[band(r), halves[h]])
            line(zz, h).start()
        r = index_of(zz, 0, 0)
        for h in range(2):
            side(r, h).wait_recv()
            add(r, halves[h], side_buf[band(r), halves[h]])

    def reduce_c(zz):
        for h in range(2):
            line(zz, h).wait_recv()
        r = index_of(zz, 0, 0)
        add(r, plain, line_buf[band(zz), :])

        @pl.when((zz >= z) & has_below)
        def _():
            sum_up(zz).wait_recv()
            add(r, plain, above_buf[band(zz), :])

        @pl.when((zz <= z) & has_above)
        def _():
            sum_down(zz).wait_recv()
            add(r, plain, below_buf[band(zz), :])

        @pl.when(zz > z)
        def _():
            sum_up(zz).start()

        @pl.when(zz < z)
        def _():
            sum_down(zz).start()

    def settle(zz):
        @pl.when((zz <= z) & has_above)
        def _():
            chain_up(zz).wait_send()

        @pl.when((zz >= z) & has_below)
        def _():
            chain_down(zz).wait_send()

        for h in range(2):
            first(zz, h).wait_send()
            second(zz, h).wait_send()
            relay(zz, h).wait_send()
        for fx, fy in corners:
            r = index_of(zz, fx, fy)
            sibling(r).wait_send()
            sibling_in(r).wait_recv()

    chunk = SQUARE * node_size * count
    column_step = next(s for s in (1792, 1024, 512, 256, 128) if width % s == 0)

    def compute(zz):
        here = pl.ds(pl.multiple_of(zz * chunk, chunk), chunk)
        lane = lax.broadcasted_iota(jnp.int32, (chunk, LANES), 1)
        marks = rows_ref[here, slice(width, width + LANES)].astype(jnp.float32)
        share = jnp.sum(jnp.where(lane == expert, marks, 0.0), axis=1, keepdims=True) / 256.0
        block = rows_ref[here, plain]
        gate = jnp.dot(block, gate_ref[...], preferred_element_type=jnp.float32)
        up = jnp.dot(block, up_ref[...], preferred_element_type=jnp.float32)
        hidden = gate / (1.0 + jnp.exp(-gate)) * up * share
        hidden = hidden.astype(jnp.bfloat16)
        for low in range(0, width, column_step):
            columns = slice(low, low + column_step)
            rows_ref[here, columns] = jnp.dot(
                hidden, down_ref[:, columns], preferred_element_type=jnp.float32
            ).astype(jnp.bfloat16)

    def expert_rows(zz):
        settle(zz)
        compute(zz)
        reduce_0(zz)

    def gather_step(t, carry):
        visit(t, gather_a)

        @pl.when(t == 0)
        def _():
            for load in loads:
                load.start()

        visit(t - 1, gather_b)
        visit(t - 3, gather_c)

        @pl.when(t == 5)
        def _():
            for load in loads:
                load.wait()

        visit(t - 5, expert_rows)
        return carry

    lax.fori_loop(0, steps + 5, gather_step, 0)

    def reduce_step(t, carry):
        q = steps - 1 - t
        visit(q, reduce_a)
        visit(q + 2, reduce_b)
        visit(q + 4, reduce_c)
        return carry

    lax.fori_loop(0, steps + 4, reduce_step, 0)
    out_ref[...] = rows_ref[own, plain]

    def reduce_end(zz, carry):
        for fx, fy in corners:
            r = index_of(zz, fx, fy)
            give(r).wait_send()
            if fy:
                side(r, 0).wait_send()
            if fx:
                side(r, 1).wait_send()
        for h in range(2):
            line(zz, h).wait_send()

        @pl.when(zz > z)
        def _():
            sum_up(zz).wait_send()

        @pl.when(zz < z)
        def _():
            sum_down(zz).wait_send()

        return carry

    lax.fori_loop(0, depth, reduce_end, 0)


def shards(rail_size, node_size, tokens, routes, route_weight, gate, up, down):
    count, width = tokens.shape
    hidden = gate.shape[-1]
    depth = rail_size // SQUARE
    total = rail_size * node_size * count
    bf16 = jnp.bfloat16
    dma = pltpu.SemaphoreType.DMA
    vmem = pl.BlockSpec(memory_space=pltpu.VMEM)
    hbm = pl.BlockSpec(memory_space=pl.ANY)
    return pl.pallas_call(
        functools.partial(body, rail_size, node_size),
        out_shape=jax.ShapeDtypeStruct((count, width), bf16),
        in_specs=[vmem] * 3 + [hbm] * 3,
        out_specs=vmem,
        scratch_shapes=[
            pltpu.VMEM((total, width + LANES), bf16),
            pltpu.VMEM((width, hidden), bf16),
            pltpu.VMEM((width, hidden), bf16),
            pltpu.VMEM((hidden, width), bf16),
            pltpu.VMEM((rail_size * count, width), bf16),
            pltpu.VMEM((rail_size * count, width), bf16),
            pltpu.VMEM((depth * count, width), bf16),
            pltpu.VMEM((depth * count, width), bf16),
            pltpu.VMEM((depth * count, width), bf16),
            dma((3,)),
            dma((2, depth)),
            dma((depth,)),
            dma((depth, 2)),
            dma((depth, 2)),
            dma((depth, 2)),
            dma((depth, 2)),
            dma((depth, 2)),
            dma((depth, 2)),
            dma((rail_size,)),
            dma((rail_size,)),
            dma((rail_size,)),
            dma((rail_size,)),
            dma((rail_size, 2)),
            dma((rail_size, 2)),
            dma((depth, 2)),
            dma((depth, 2)),
            dma((depth,)),
            dma((depth,)),
            dma((depth,)),
        ],
        compiler_params=pltpu.CompilerParams(
            collective_id=0, has_side_effects=True, vmem_limit_bytes=56 * 1024 * 1024
        ),
        cost_estimate=pl.CostEstimate(
            flops=6 * total * width * hidden,
            bytes_accessed=6 * width * hidden,
            transcendentals=total * hidden,
        ),
    )(tokens, routes.T, route_weight.T, gate, up, down)


def solution(mesh):
    in_specs = (
        P(("groups", "rail", "node"), None),
        P(("groups", "rail", "node"), None),
        P(("groups", "rail", "node"), None),
        P("rail", "node", None, None),
        P("rail", "node", None, None),
        P("rail", "node", None, None),
    )
    out_specs = P(("groups", "rail", "node"), None)
    work = functools.partial(shards, mesh.shape["rail"], mesh.shape["node"])
    return jax.shard_map(work, mesh=mesh, in_specs=in_specs, out_specs=out_specs, check_vma=False)
```

```python
import functools

import jax
import jax.numpy as jnp
from jax import lax
from jax.experimental import pallas as pl
from jax.experimental.pallas import tpu as pltpu
from jax.sharding import PartitionSpec as P

SLICES = 8
SQUARE = 4
LANES = 128


def body(
    rail_size,
    node_size,
    tokens_ref,
    routes_ref,
    weight_ref,
    gate_hbm,
    up_hbm,
    down_hbm,
    out_ref,
    rows_ref,
    gate_ref,
    up_ref,
    down_ref,
    sib_buf,
    side_buf,
    line_buf,
    above_buf,
    below_buf,
    load_sem,
    chain_send,
    chain_recv,
    first_send,
    first_recv,
    second_send,
    second_recv,
    relay_send,
    relay_recv,
    sib_send,
    sib_recv,
    give_send,
    give_recv,
    side_send,
    side_recv,
    line_send,
    line_recv,
    sum_send,
    above_recv,
    below_recv,
):
    count, width = tokens_ref.shape
    middle = width // LANES // 2 * LANES
    depth = rail_size // SQUARE
    rail = lax.axis_index("rail")
    node = lax.axis_index("node")
    x, y, z = lax.rem(rail, 2), lax.rem(rail // 2, 2), rail // SQUARE
    expert = rail // SLICES * node_size + node
    to_sib = {"node": 1 - node}
    to_x = {"rail": rail + 1 - 2 * x}
    to_y = {"rail": rail + 2 - 4 * y}
    to_above = {"rail": rail + SQUARE}
    to_below = {"rail": rail - SQUARE}
    has_above = z < depth - 1
    has_below = z > 0
    steps = 2 * depth - 1

    def index_of(zz, flip_x, flip_y):
        xx = 1 - x if flip_x else x
        yy = 1 - y if flip_y else y
        return zz * SQUARE + yy * 2 + xx

    def band(i):
        return pl.ds(pl.multiple_of(i * count, count), count)

    full = slice(0, width + LANES)
    plain = slice(0, width)
    halves_wide = (slice(0, middle), slice(middle, width + LANES))
    halves = (slice(0, middle), slice(middle, width))

    def rows_at(r, n, columns):
        return rows_ref.at[band(r * node_size + n), columns]

    def copy(src, dst, send, recv, target):
        return pltpu.make_async_remote_copy(
            src_ref=src,
            dst_ref=dst,
            send_sem=send,
            recv_sem=recv,
            device_id=target,
            device_id_type=pl.DeviceIdType.MESH,
        )

    loads = [
        pltpu.make_async_copy(hbm.at[0, 0], ref, load_sem.at[i])
        for i, (hbm, ref) in enumerate(
            ((gate_hbm, gate_ref), (up_hbm, up_ref), (down_hbm, down_ref))
        )
    ]

    barrier = pltpu.get_barrier_semaphore()
    for target in (to_sib, to_x, to_y):
        pl.semaphore_signal(barrier, inc=1, device_id=target, device_id_type=pl.DeviceIdType.MESH)

    @pl.when(has_above)
    def _():
        pl.semaphore_signal(
            barrier, inc=1, device_id=to_above, device_id_type=pl.DeviceIdType.MESH
        )

    @pl.when(has_below)
    def _():
        pl.semaphore_signal(
            barrier, inc=1, device_id=to_below, device_id_type=pl.DeviceIdType.MESH
        )

    own = band(rail * node_size + node)
    rows_ref[own, plain] = tokens_ref[...]
    kind = lax.broadcasted_iota(jnp.int32, (LANES, count), 0)
    table = jnp.zeros((LANES, count), jnp.float32)
    for k in range(routes_ref.shape[0]):
        table += jnp.where(
            kind == routes_ref[k : k + 1, :], weight_ref[k : k + 1, :].astype(jnp.float32), 0.0
        )
    unit = lax.broadcasted_iota(jnp.int32, (count, count), 0) == lax.broadcasted_iota(
        jnp.int32, (count, count), 1
    )
    named = lax.dot_general(
        unit.astype(jnp.bfloat16),
        table.astype(jnp.bfloat16),
        (((1,), (1,)), ((), ())),
        preferred_element_type=jnp.float32,
    )
    rows_ref[own, slice(width, width + LANES)] = named.astype(jnp.bfloat16)
    pl.semaphore_wait(barrier, 3 + has_above.astype(jnp.int32) + has_below.astype(jnp.int32))

    def place(q):
        half = (q + 1) // 2
        return jnp.where(lax.rem(q, 2) == 1, z - half, z + half)

    def visit(q, work):
        zz = place(q)

        @pl.when((q >= 0) & (q < steps) & (zz >= 0) & (zz < depth))
        def _():
            work(zz)

    def chain_up(zz):
        piece = rows_at(index_of(zz, 0, 0), node, full)
        return copy(piece, piece, chain_send.at[0, zz], chain_recv.at[zz], to_above)

    def chain_down(zz):
        piece = rows_at(index_of(zz, 0, 0), node, full)
        return copy(piece, piece, chain_send.at[1, zz], chain_recv.at[zz], to_below)

    def first(zz, h):
        piece = rows_at(index_of(zz, 0, 0), node, halves_wide[h])
        return copy(
            piece, piece, first_send.at[zz, h], first_recv.at[zz, h], (to_x, to_y)[h]
        )

    def first_in(zz, h):
        piece = rows_at(index_of(zz, h == 0, h == 1), node, halves_wide[h])
        return copy(
            piece, piece, first_send.at[zz, h], first_recv.at[zz, h], (to_x, to_y)[h]
        )

    def second(zz, h):
        piece = rows_at(index_of(zz, 0, 0), node, halves_wide[h])
        return copy(
            piece, piece, second_send.at[zz, h], second_recv.at[zz, h], (to_y, to_x)[h]
        )

    def second_in(zz, h):
        piece = rows_at(index_of(zz, h == 1, h == 0), node, halves_wide[h])
        return copy(
            piece, piece, second_send.at[zz, h], second_recv.at[zz, h], (to_y, to_x)[h]
        )

    def relay(zz, h):
        piece = rows_at(index_of(zz, h == 0, h == 1), node, halves_wide[h])
        return copy(
            piece, piece, relay_send.at[zz, h], relay_recv.at[zz, h], (to_y, to_x)[h]
        )

    def relay_in(zz, h):
        piece = rows_at(index_of(zz, 1, 1), node, halves_wide[h])
        return copy(
            piece, piece, relay_send.at[zz, h], relay_recv.at[zz, h], (to_y, to_x)[h]
        )

    def sibling(r):
        piece = rows_at(r, node, full)
        return copy(piece, piece, sib_send.at[r], sib_recv.at[r], to_sib)

    def sibling_in(r):
        piece = rows_at(r, 1 - node, full)
        return copy(piece, piece, sib_send.at[r], sib_recv.at[r], to_sib)

    def gather_a(zz):
        @pl.when(zz != z)
        def _():
            chain_up(zz).wait_recv()

        @pl.when((zz <= z) & has_above)
        def _():
            chain_up(zz).start()

        @pl.when((zz >= z) & has_below)
        def _():
            chain_down(zz).start()

        for h in range(2):
            first(zz, h).start()
        for h in range(2):
            second(zz, h).start()
        sibling(index_of(zz, 0, 0)).start()

    def gather_b(zz):
        for h in range(2):
            first_in(zz, h).wait_recv()
            relay(zz, h).start()

    def gather_c(zz):
        for h in range(2):
            second_in(zz, h).wait_recv()
        sibling(index_of(zz, 0, 1)).start()
        sibling(index_of(zz, 1, 0)).start()
        for h in range(2):
            relay_in(zz, h).wait_recv()
        sibling(index_of(zz, 1, 1)).start()

    def give(r):
        return copy(
            rows_at(r, 1 - node, plain),
            sib_buf.at[band(r), :],
            give_send.at[r],
            give_recv.at[r],
            to_sib,
        )

    def side(r, h):
        return copy(
            rows_at(r, node, halves[h]),
            side_buf.at[band(r), halves[h]],
            side_send.at[r, h],
            side_recv.at[r, h],
            (to_y, to_x)[h],
        )

    def line(zz, h):
        return copy(
            rows_at(index_of(zz, h == 0, h == 1), node, halves[h]),
            line_buf.at[band(zz), halves[h]],
            line_send.at[zz, h],
            line_recv.at[zz, h],
            (to_x, to_y)[h],
        )

    def sum_up(zz):
        return copy(
            rows_at(index_of(zz, 0, 0), node, plain),
            above_buf.at[band(zz), :],
            sum_send.at[zz],
            above_recv.at[zz],
            to_above,
        )

    def sum_down(zz):
        return copy(
            rows_at(index_of(zz, 0, 0), node, plain),
            below_buf.at[band(zz), :],
            sum_send.at[zz],
            below_recv.at[zz],
            to_below,
        )

    def add(r, columns, other):
        where = band(r * node_size + node)
        rows_ref[where, columns] = (
            rows_ref[where, columns].astype(jnp.float32) + other.astype(jnp.float32)
        ).astype(jnp.bfloat16)

    corners = ((1, 1), (0, 1), (1, 0), (0, 0))

    def reduce_0(zz):
        for fx, fy in corners:
            give(index_of(zz, fx, fy)).start()

    def reduce_a(zz):
        for fx, fy in corners:
            r = index_of(zz, fx, fy)
            give(r).wait_recv()
            add(r, plain, sib_buf[band(r), :])
            if fy:
                side(r, 0).start()
            if fx:
                side(r, 1).start()

    def reduce_b(zz):
        for h in range(2):
            r = index_of(zz, h == 0, h == 1)
            side(r, h).wait_recv()
            add(r, halves[h], side_buf[band(r), halves[h]])
            line(zz, h).start()
        r = index_of(zz, 0, 0)
        for h in range(2):
            side(r, h).wait_recv()
            add(r, halves[h], side_buf[band(r), halves[h]])

    def reduce_c(zz):
        for h in range(2):
            line(zz, h).wait_recv()
        r = index_of(zz, 0, 0)
        add(r, plain, line_buf[band(zz), :])

        @pl.when((zz >= z) & has_below)
        def _():
            sum_up(zz).wait_recv()
            add(r, plain, above_buf[band(zz), :])

        @pl.when((zz <= z) & has_above)
        def _():
            sum_down(zz).wait_recv()
            add(r, plain, below_buf[band(zz), :])

        @pl.when(zz > z)
        def _():
            sum_up(zz).start()

        @pl.when(zz < z)
        def _():
            sum_down(zz).start()

    def settle(zz):
        @pl.when((zz <= z) & has_above)
        def _():
            chain_up(zz).wait_send()

        @pl.when((zz >= z) & has_below)
        def _():
            chain_down(zz).wait_send()

        for h in range(2):
            first(zz, h).wait_send()
            second(zz, h).wait_send()
            relay(zz, h).wait_send()
        for fx, fy in corners:
            r = index_of(zz, fx, fy)
            sibling(r).wait_send()
            sibling_in(r).wait_recv()

    chunk = SQUARE * node_size * count
    column_step = next(s for s in (1792, 1024, 512, 256, 128) if width % s == 0)

    def compute(zz):
        here = pl.ds(pl.multiple_of(zz * chunk, chunk), chunk)
        lane = lax.broadcasted_iota(jnp.int32, (chunk, LANES), 1)
        marks = rows_ref[here, slice(width, width + LANES)].astype(jnp.float32)
        share = jnp.sum(jnp.where(lane == expert, marks, 0.0), axis=1, keepdims=True) / 256.0
        block = rows_ref[here, plain]
        gate = jnp.dot(block, gate_ref[...], preferred_element_type=jnp.float32)
        up = jnp.dot(block, up_ref[...], preferred_element_type=jnp.float32)
        hidden = gate / (1.0 + jnp.exp(-gate)) * up * share
        hidden = hidden.astype(jnp.bfloat16)
        for low in range(0, width, column_step):
            columns = slice(low, low + column_step)
            rows_ref[here, columns] = jnp.dot(
                hidden, down_ref[:, columns], preferred_element_type=jnp.float32
            ).astype(jnp.bfloat16)

    def expert_rows(zz):
        settle(zz)
        compute(zz)
        reduce_0(zz)

    def gather_step(t, carry):
        visit(t, gather_a)

        @pl.when(t == 0)
        def _():
            for load in loads:
                load.start()

        visit(t - 1, gather_b)
        visit(t - 3, gather_c)

        @pl.when(t == 5)
        def _():
            for load in loads:
                load.wait()

        visit(t - 5, expert_rows)
        return carry

    lax.fori_loop(0, steps + 5, gather_step, 0)

    def reduce_step(t, carry):
        q = steps - 1 - t
        visit(q, reduce_a)
        visit(q + 4, reduce_c)
        visit(q + 2, reduce_b)
        return carry

    lax.fori_loop(0, steps + 4, reduce_step, 0)
    out_ref[...] = rows_ref[own, plain]

    def reduce_end(zz, carry):
        for fx, fy in corners:
            r = index_of(zz, fx, fy)
            give(r).wait_send()
            if fy:
                side(r, 0).wait_send()
            if fx:
                side(r, 1).wait_send()
        for h in range(2):
            line(zz, h).wait_send()

        @pl.when(zz > z)
        def _():
            sum_up(zz).wait_send()

        @pl.when(zz < z)
        def _():
            sum_down(zz).wait_send()

        return carry

    lax.fori_loop(0, depth, reduce_end, 0)


def shards(rail_size, node_size, tokens, routes, route_weight, gate, up, down):
    count, width = tokens.shape
    hidden = gate.shape[-1]
    depth = rail_size // SQUARE
    total = rail_size * node_size * count
    bf16 = jnp.bfloat16
    dma = pltpu.SemaphoreType.DMA
    vmem = pl.BlockSpec(memory_space=pltpu.VMEM)
    hbm = pl.BlockSpec(memory_space=pl.ANY)
    return pl.pallas_call(
        functools.partial(body, rail_size, node_size),
        out_shape=jax.ShapeDtypeStruct((count, width), bf16),
        in_specs=[vmem] * 3 + [hbm] * 3,
        out_specs=vmem,
        scratch_shapes=[
            pltpu.VMEM((total, width + LANES), bf16),
            pltpu.VMEM((width, hidden), bf16),
            pltpu.VMEM((width, hidden), bf16),
            pltpu.VMEM((hidden, width), bf16),
            pltpu.VMEM((rail_size * count, width), bf16),
            pltpu.VMEM((rail_size * count, width), bf16),
            pltpu.VMEM((depth * count, width), bf16),
            pltpu.VMEM((depth * count, width), bf16),
            pltpu.VMEM((depth * count, width), bf16),
            dma((3,)),
            dma((2, depth)),
            dma((depth,)),
            dma((depth, 2)),
            dma((depth, 2)),
            dma((depth, 2)),
            dma((depth, 2)),
            dma((depth, 2)),
            dma((depth, 2)),
            dma((rail_size,)),
            dma((rail_size,)),
            dma((rail_size,)),
            dma((rail_size,)),
            dma((rail_size, 2)),
            dma((rail_size, 2)),
            dma((depth, 2)),
            dma((depth, 2)),
            dma((depth,)),
            dma((depth,)),
            dma((depth,)),
        ],
        compiler_params=pltpu.CompilerParams(
            collective_id=0, has_side_effects=True, vmem_limit_bytes=56 * 1024 * 1024
        ),
        cost_estimate=pl.CostEstimate(
            flops=6 * total * width * hidden,
            bytes_accessed=6 * width * hidden,
            transcendentals=total * hidden,
        ),
    )(tokens, routes.T, route_weight.T, gate, up, down)


def solution(mesh):
    in_specs = (
        P(("groups", "rail", "node"), None),
        P(("groups", "rail", "node"), None),
        P(("groups", "rail", "node"), None),
        P("rail", "node", None, None),
        P("rail", "node", None, None),
        P("rail", "node", None, None),
    )
    out_specs = P(("groups", "rail", "node"), None)
    work = functools.partial(shards, mesh.shape["rail"], mesh.shape["node"])
    return jax.shard_map(work, mesh=mesh, in_specs=in_specs, out_specs=out_specs, check_vma=False)
```
